32 devices in a mesh: space: 8 (over y, x, core), snap: 4 (over z).
Axes of the slice: x: 2, y: 2, z: 4, core: 2. Of those that a mesh axis runs over, the one named last changes fastest.
Arguments:
- snapshots: float32 [32768, 512], P('space', 'snap')
- picks: int32 [2, 128], replicated, may hold values from 0 to 511, as said below
Outputs:
- residual: float32 [32768, 512], P('space', 'snap')
- basis_scaled: float32 [32768, 256], P('space')
The draws below stay inside these ranges and needn't reach their ends.
Inputs may be any that keep to these rules, and one draw needn't show every extreme that they name: All entries of picks are distinct over both dimensions.
All inputs are finite; a program needn't handle non-finite values.
Results may differ from the reference program's by a relative error of at most 0.0003.
Values sent between devices are 32-bit elements; how exact they have to be, the bound alone decides.
A program may use at most 64 MiB of HBM per device.

```python
import math
import jax
import jax.numpy as jnp
from jax import lax

NSNAP = 512
PANEL = 128
STEPS = 2
NODES = 32768


def draw_snapshots(key, part):
    keys = jax.random.split(jax.random.fold_in(key, 11), 4)
    modes = jax.random.normal(keys[0], (NODES, 8), jnp.float32)
    mixing = jax.random.normal(keys[1], (8, NSNAP), jnp.float32)
    common = jnp.zeros((NODES, NSNAP), jnp.float32)
    for index in range(8):
        common = common + modes[:, index:index + 1] * mixing[index:index + 1, :]
    row_scale = jnp.exp(jax.random.uniform(keys[3], (NODES, 1), jnp.float32) * math.log(4.0) - math.log(2.0))
    noise = jax.random.normal(keys[2], (NODES, NSNAP), jnp.float32) * 0.5
    common = common * 0.4
    return (row_scale * (common + noise)).astype(jnp.float32)


def draw_picks(key, part):
    keys = jax.random.split(jax.random.fold_in(key, 23), 2)
    column = jnp.arange(NSNAP, dtype=jnp.int32)
    weight = 1 + column * 4 // NSNAP
    raw = jax.random.randint(keys[0], (NSNAP,), 0, 2 ** 19, dtype=jnp.int32) * weight
    scores = raw * NSNAP + column
    forced = (column == 0) | (column == NSNAP - 1)
    scores = jnp.where(forced, 2 ** 30 + column, scores)
    values, chosen = jax.lax.top_k(scores, STEPS * PANEL)
    chosen = jax.random.permutation(keys[1], chosen.astype(jnp.int32))
    return chosen.reshape(STEPS, PANEL).astype(jnp.int32)


def setup_inputs(seed: int = 0) -> dict:
    key_of = jax.random.split(jax.random.key(seed), 3)
    snapshots = draw_snapshots(jax.random.fold_in(key_of[2], 71), 0)
    picks = draw_picks(jax.random.fold_in(key_of[2], 71), 0)
    return dict(snapshots=snapshots, picks=picks)


def hdot(left, right):
    return jnp.dot(left.astype(jnp.float32), right.astype(jnp.float32), precision=lax.Precision.HIGHEST, preferred_element_type=jnp.float32)

def reference(snapshots, picks):
    residual = snapshots
    basis = None
    for step in range(STEPS):
        panel = jnp.take(snapshots, picks[step].astype(jnp.int32), axis=1)
        if basis is not None:
            coef = hdot(basis.T, panel)
            panel = panel - hdot(basis, coef)
        gram = hdot(panel.T, panel)
        lower = jnp.linalg.cholesky(gram)
        fresh = jax.scipy.linalg.solve_triangular(lower, panel.T, lower=True).T
        weights = hdot(fresh.T, residual)
        residual = residual - hdot(fresh, weights)
        basis = fresh if basis is None else jnp.concatenate([basis, fresh], axis=1)
    return (residual, basis * math.sqrt(NODES))
```

```python
import functools
import math

import jax
import jax.numpy as jnp
from jax import lax
from jax.experimental import pallas as pl
from jax.experimental.pallas import tpu as pltpu
from jax.sharding import PartitionSpec as P

MESH = pl.DeviceIdType.MESH
HIGHEST = lax.Precision.HIGHEST
LANES = 128


def dot(left, right, contract=((1,), (0,))):
    return lax.dot_general(
        left, right, (contract, ((), ())), precision=HIGHEST, preferred_element_type=jnp.float32
    )


def gather_kernel(
    spaces, snaps, chunk, block,
    x_ref, sel_ref, panel_ref, total_ref,
    own, acc, gram, parts,
    send_sem, recv_sem, gs_sem, gr_sem, bs_sem, br_sem,
):
    me = lax.axis_index("space")
    z = lax.axis_index("snap")
    rows = x_ref.shape[0]
    count = rows // chunk
    lag = min(2, count)
    early = z // (snaps // 2)
    late = 1 - early

    barrier = pltpu.get_barrier_semaphore()
    for k in range(1, spaces):
        pl.semaphore_signal(
            barrier, inc=1, device_id={"space": lax.rem(me + k, spaces)}, device_id_type=MESH
        )
    for k in range(1, snaps):
        pl.semaphore_signal(
            barrier, inc=1, device_id={"snap": lax.rem(z + k, snaps)}, device_id_type=MESH
        )
    pl.semaphore_wait(barrier, spaces + snaps - 2)

    def span(c):
        return pl.ds(pl.multiple_of(c * chunk, chunk), chunk)

    def place(d):
        return z + d * (snaps - 1 - 2 * z)

    def hop(d, c):
        return pltpu.make_async_remote_copy(
            src_ref=acc.at[d, span(c)],
            dst_ref=acc.at[d, span(c)],
            send_sem=send_sem.at[d, c],
            recv_sem=recv_sem.at[d, c],
            device_id={"snap": lax.rem(z + 1 - 2 * d + snaps, snaps)},
            device_id_type=MESH,
        )

    def prepare(c, carry):
        mine = dot(x_ref[span(c), :], sel_ref[...])
        own[span(c), :] = mine

        @pl.when(place(early) == 0)
        def _():
            acc[early, span(c), :] = mine
            hop(early, c).start()

        return carry

    lax.fori_loop(0, count, prepare, 0)
    gram[...] = jnp.zeros_like(gram)

    def relay(c):
        @pl.when(place(early) > 0)
        def _():
            hop(early, c).wait_recv()
            acc[early, span(c), :] = acc[early, span(c), :] + own[span(c), :]
            hop(early, c).start()

    def finish(c):
        hop(late, c).wait_recv()
        panel = acc[late, span(c), :] + acc[early, span(c), :]
        panel_ref[span(c), :] = panel

        @pl.when(place(late) < snaps - 1)
        def _():
            acc[late, span(c), :] = acc[late, span(c), :] + own[span(c), :]
            hop(late, c).start()

        half = panel.shape[1] // 2
        first, second = panel[:, :half], panel[:, half:]
        wide = jnp.concatenate([first, x_ref[span(c), :]], axis=1)
        both = dot(panel, wide, ((0,), (0,)))
        gram[0:2 * half, :] += both[:, :half]
        gram[2 * half:4 * half, :] += both[:, half:]
        gram[4 * half:5 * half, :] += dot(second, second, ((0,), (0,)))

    for c in range(lag):
        relay(c)

    def step(c, carry):
        relay(c)
        finish(c - lag)
        return carry

    lax.fori_loop(lag, count, step, 0)
    for c in range(count - lag, count):
        finish(c)

    def owned(k):
        return pl.ds(pl.multiple_of(k * block, block), block)

    def scatter(k):
        peer = lax.rem(me + k, spaces)
        return pltpu.make_async_remote_copy(
            src_ref=gram.at[owned(peer)],
            dst_ref=parts.at[k],
            send_sem=gs_sem.at[k],
            recv_sem=gr_sem.at[k],
            device_id={"space": peer},
            device_id_type=MESH,
        )

    def spread(k):
        return pltpu.make_async_remote_copy(
            src_ref=total_ref.at[owned(me)],
            dst_ref=total_ref.at[owned(me)],
            send_sem=bs_sem.at[k],
            recv_sem=br_sem.at[k],
            device_id={"space": lax.rem(me + k, spaces)},
            device_id_type=MESH,
        )

    for k in range(1, spaces):
        scatter(k).start()
    mine = gram[owned(me), :]
    for k in range(1, spaces):
        scatter(k).wait_recv()
        mine = mine + parts[k]
    total_ref[owned(me), :] = mine
    for k in range(1, spaces):
        spread(k).start()
    for k in range(1, spaces):
        source = lax.rem(me - k + spaces, spaces)
        pltpu.make_async_remote_copy(
            src_ref=total_ref.at[owned(me)],
            dst_ref=total_ref.at[owned(source)],
            send_sem=bs_sem.at[k],
            recv_sem=br_sem.at[k],
            device_id={"space": lax.rem(me + k, spaces)},
            device_id_type=MESH,
        ).wait_recv()
    for k in range(1, spaces):
        scatter(k).wait_send()
        spread(k).wait_send()

    def drain(c, carry):
        hop(early, c).wait_send()

        @pl.when(place(late) < snaps - 1)
        def _():
            hop(late, c).wait_send()

        return carry

    lax.fori_loop(0, count, drain, 0)


def gather(x, sel, spaces, snaps, chunk):
    rows, wide = x.shape[0], sel.shape[1]
    count = rows // chunk
    height = 5 * wide // 2
    block = -(-height // (8 * spaces)) * 8
    return pl.pallas_call(
        functools.partial(gather_kernel, spaces, snaps, chunk, block),
        out_shape=(
            jax.ShapeDtypeStruct((rows, wide), jnp.float32),
            jax.ShapeDtypeStruct((spaces * block, LANES), jnp.float32),
        ),
        in_specs=[pl.BlockSpec(memory_space=pltpu.VMEM)] * 2,
        out_specs=[pl.BlockSpec(memory_space=pltpu.VMEM)] * 2,
        scratch_shapes=[
            pltpu.VMEM((rows, wide), jnp.float32),
            pltpu.VMEM((2, rows, wide), jnp.float32),
            pltpu.VMEM((spaces * block, LANES), jnp.float32),
            pltpu.VMEM((spaces, block, LANES), jnp.float32),
            pltpu.SemaphoreType.DMA((2, count)),
            pltpu.SemaphoreType.DMA((2, count)),
            pltpu.SemaphoreType.DMA((spaces,)),
            pltpu.SemaphoreType.DMA((spaces,)),
            pltpu.SemaphoreType.DMA((spaces,)),
            pltpu.SemaphoreType.DMA((spaces,)),
        ],
        compiler_params=pltpu.CompilerParams(
            collective_id=0, has_side_effects=True, vmem_limit_bytes=40 * 2 ** 20
        ),
        name="gather_panel",
    )(x, sel)


def inverse_factor(square, out):
    size = square.shape[0]
    groups = size // 8
    left = [square[8 * g:8 * g + 8, :] for g in range(groups)]
    lane = lax.broadcasted_iota(jnp.int32, (8, size), 1)
    row = lax.broadcasted_iota(jnp.int32, (8, size), 0)
    right = [(lane == row + 8 * g).astype(jnp.float32) for g in range(groups)]
    for j in range(size):
        g, s = divmod(j, 8)
        pivot = left[g][s:s + 1, j:j + 1]
        line = left[g][s:s + 1, :] / pivot
        unit = right[g][s:s + 1, :]
        out[j:j + 1, :] = unit / jnp.sqrt(pivot)
        unit = unit / pivot
        for b in range(g, groups):
            if b == g and s == 7:
                continue
            factor = jnp.broadcast_to(left[b][:, j:j + 1], (8, size))
            if b == g:
                factor = jnp.where(row > s, factor, 0.0)
            left[b] = left[b] - factor * line
            right[b] = right[b] - factor * unit


def finish_kernel(scale, total_ref, panel_ref, x_ref, res_ref, basis_ref, inv1, inv2, inv, weights):
    @pl.when(pl.program_id(0) == 0)
    def _():
        n = LANES
        inverse_factor(total_ref[0:n, :], inv1)
        first = inv1[...]
        low = dot(total_ref[n:2 * n, :], first, ((1,), (1,)))
        rest = total_ref[4 * n:5 * n, :] - dot(low, low, ((1,), (1,)))
        inverse_factor(rest, inv2)
        second = inv2[...]
        inv[0:n, 0:n] = first
        inv[0:n, n:2 * n] = jnp.zeros((n, n), jnp.float32)
        inv[n:2 * n, 0:n] = -dot(second, dot(low, first))
        inv[n:2 * n, n:2 * n] = second
        weights[...] = dot(inv[...], total_ref[2 * n:4 * n, :])

    fresh = dot(panel_ref[...], inv[...], ((1,), (1,)))
    basis_ref[...] = fresh * scale
    res_ref[...] = x_ref[...] - dot(fresh, weights[...])


def finish(total, panel, x, scale, tile):
    rows, wide = panel.shape
    return pl.pallas_call(
        functools.partial(finish_kernel, scale),
        grid=(rows // tile,),
        out_shape=(
            jax.ShapeDtypeStruct(x.shape, jnp.float32),
            jax.ShapeDtypeStruct(panel.shape, jnp.float32),
        ),
        in_specs=[
            pl.BlockSpec(total.shape, lambda i: (0, 0)),
            pl.BlockSpec((tile, wide), lambda i: (i, 0)),
            pl.BlockSpec((tile, x.shape[1]), lambda i: (i, 0)),
        ],
        out_specs=[
            pl.BlockSpec((tile, x.shape[1]), lambda i: (i, 0)),
            pl.BlockSpec((tile, wide), lambda i: (i, 0)),
        ],
        scratch_shapes=[
            pltpu.VMEM((LANES, LANES), jnp.float32),
            pltpu.VMEM((LANES, LANES), jnp.float32),
            pltpu.VMEM((2 * LANES, 2 * LANES), jnp.float32),
            pltpu.VMEM((2 * LANES, LANES), jnp.float32),
        ],
        compiler_params=pltpu.CompilerParams(vmem_limit_bytes=24 * 2 ** 20),
        name="finish_basis",
    )(total, panel, x)


def solution(mesh):
    spaces, snaps = mesh.shape["space"], mesh.shape["snap"]

    def on_device(x, picks):
        rows, cols = x.shape
        column = jnp.arange(cols, dtype=jnp.int32) + lax.axis_index("snap") * cols
        sel = (column[:, None] == picks.reshape(1, -1)).astype(jnp.float32)
        panel, total = gather(x, sel, spaces, snaps, 256)
        return finish(total, panel, x, math.sqrt(rows * spaces), 512)

    return jax.shard_map(
        on_device,
        mesh=mesh,
        in_specs=(P("space", "snap"), P()),
        out_specs=(P("space", "snap"), P("space", None)),
        check_vma=False,
    )
```

```python
import functools
import math

import jax
import jax.numpy as jnp
from jax import lax
from jax.experimental import pallas as pl
from jax.experimental.pallas import tpu as pltpu
from jax.sharding import PartitionSpec as P

MESH = pl.DeviceIdType.MESH
HIGHEST = lax.Precision.HIGHEST
LANES = 128


def dot(left, right, contract=((1,), (0,))):
    return lax.dot_general(
        left, right, (contract, ((), ())), precision=HIGHEST, preferred_element_type=jnp.float32
    )


def gather_kernel(
    spaces, snaps, chunk, block,
    x_ref, picks_ref, panel_ref, total_ref,
    own, acc, gram, parts,
    send_sem, recv_sem, gs_sem, gr_sem, bs_sem, br_sem,
):
    me = lax.axis_index("space")
    z = lax.axis_index("snap")
    rows = x_ref.shape[0]
    count = rows // chunk
    cols = x_ref.shape[1]
    column = lax.broadcasted_iota(jnp.int32, (cols, picks_ref.shape[1]), 0) + z * cols
    chosen = (column == picks_ref[...]).astype(jnp.float32)
    early = z // (snaps // 2)
    late = 1 - early

    barrier = pltpu.get_barrier_semaphore()
    for k in range(1, spaces):
        pl.semaphore_signal(
            barrier, inc=1, device_id={"space": lax.rem(me + k, spaces)}, device_id_type=MESH
        )
    for k in range(1, snaps):
        pl.semaphore_signal(
            barrier, inc=1, device_id={"snap": lax.rem(z + k, snaps)}, device_id_type=MESH
        )
    pl.semaphore_wait(barrier, spaces + snaps - 2)

    def span(c):
        return pl.ds(pl.multiple_of(c * chunk, chunk), chunk)

    def place(d):
        return z + d * (snaps - 1 - 2 * z)

    def hop(d, c):
        return pltpu.make_async_remote_copy(
            src_ref=acc.at[d, span(c)],
            dst_ref=acc.at[d, span(c)],
            send_sem=send_sem.at[d, c],
            recv_sem=recv_sem.at[d, c],
            device_id={"snap": lax.rem(z + 1 - 2 * d + snaps, snaps)},
            device_id_type=MESH,
        )

    def prepare(c, carry):
        mine = dot(x_ref[span(c), :], chosen)
        own[span(c), :] = mine

        @pl.when(place(early) == 0)
        def _():
            acc[early, span(c), :] = mine
            hop(early, c).start()

        return carry

    lax.fori_loop(0, count, prepare, 0)
    gram[...] = jnp.zeros_like(gram)

    def relay(c):
        @pl.when(place(early) > 0)
        def _():
            hop(early, c).wait_recv()
            acc[early, span(c), :] = acc[early, span(c), :] + own[span(c), :]
            hop(early, c).start()

    def join(c):
        hop(late, c).wait_recv()
        came = acc[late, span(c), :]
        panel_ref[span(c), :] = came + acc[early, span(c), :]

        @pl.when(place(late) < snaps - 1)
        def _():
            acc[late, span(c), :] = came + own[span(c), :]
            hop(late, c).start()

    def square(pair):
        where = pl.ds(pl.multiple_of(pair * 2 * chunk, 2 * chunk), 2 * chunk)
        panel = panel_ref[where, :]
        half = panel.shape[1] // 2
        first, second = panel[:, :half], panel[:, half:]
        wide = jnp.concatenate([first, x_ref[where, :]], axis=1)
        both = dot(panel, wide, ((0,), (0,)))
        gram[0:2 * half, :] += both[:, :half]
        gram[2 * half:4 * half, :] += both[:, half:]
        gram[4 * half:5 * half, :] += dot(second, second, ((0,), (0,)))

    for c in range(4):
        relay(c)
    join(0)

    def step(t, carry):
        relay(2 * t)
        join(2 * t - 3)
        square(t - 2)
        relay(2 * t + 1)
        join(2 * t - 2)
        return carry

    lax.fori_loop(2, count // 2, step, 0)
    join(count - 3)
    square(count // 2 - 2)
    join(count - 2)
    join(count - 1)
    square(count // 2 - 1)

    def owned(k):
        return pl.ds(pl.multiple_of(k * block, block), block)

    def scatter(k):
        peer = lax.rem(me + k, spaces)
        return pltpu.make_async_remote_copy(
            src_ref=gram.at[owned(peer)],
            dst_ref=parts.at[k],
            send_sem=gs_sem.at[k],
            recv_sem=gr_sem.at[k],
            device_id={"space": peer},
            device_id_type=MESH,
        )

    def spread(k):
        return pltpu.make_async_remote_copy(
            src_ref=total_ref.at[owned(me)],
            dst_ref=total_ref.at[owned(me)],
            send_sem=bs_sem.at[k],
            recv_sem=br_sem.at[k],
            device_id={"space": lax.rem(me + k, spaces)},
            device_id_type=MESH,
        )

    for k in range(1, spaces):
        scatter(k).start()
    mine = gram[owned(me), :]
    for k in range(1, spaces):
        scatter(k).wait_recv()
        mine = mine + parts[k]
    total_ref[owned(me), :] = mine
    for k in range(1, spaces):
        spread(k).start()
    for k in range(1, spaces):
        source = lax.rem(me - k + spaces, spaces)
        pltpu.make_async_remote_copy(
            src_ref=total_ref.at[owned(me)],
            dst_ref=total_ref.at[owned(source)],
            send_sem=bs_sem.at[k],
            recv_sem=br_sem.at[k],
            device_id={"space": lax.rem(me + k, spaces)},
            device_id_type=MESH,
        ).wait_recv()
    for k in range(1, spaces):
        scatter(k).wait_send()
        spread(k).wait_send()

    def drain(c, carry):
        hop(early, c).wait_send()

        @pl.when(place(late) < snaps - 1)
        def _():
            hop(late, c).wait_send()

        return carry

    lax.fori_loop(0, count, drain, 0)


def gather(x, picks, spaces, snaps, chunk):
    rows, wide = x.shape[0], picks.shape[1]
    count = rows // chunk
    height = 5 * wide // 2
    block = -(-height // (8 * spaces)) * 8
    return pl.pallas_call(
        functools.partial(gather_kernel, spaces, snaps, chunk, block),
        out_shape=(
            jax.ShapeDtypeStruct((rows, wide), jnp.float32),
            jax.ShapeDtypeStruct((spaces * block, LANES), jnp.float32),
        ),
        in_specs=[pl.BlockSpec(memory_space=pltpu.VMEM)] * 2,
        out_specs=[pl.BlockSpec(memory_space=pltpu.VMEM)] * 2,
        scratch_shapes=[
            pltpu.VMEM((rows, wide), jnp.float32),
            pltpu.VMEM((2, rows, wide), jnp.float32),
            pltpu.VMEM((spaces * block, LANES), jnp.float32),
            pltpu.VMEM((spaces, block, LANES), jnp.float32),
            pltpu.SemaphoreType.DMA((2, count)),
            pltpu.SemaphoreType.DMA((2, count)),
            pltpu.SemaphoreType.DMA((spaces,)),
            pltpu.SemaphoreType.DMA((spaces,)),
            pltpu.SemaphoreType.DMA((spaces,)),
            pltpu.SemaphoreType.DMA((spaces,)),
        ],
        compiler_params=pltpu.CompilerParams(
            collective_id=0, has_side_effects=True, vmem_limit_bytes=40 * 2 ** 20
        ),
        name="gather_panel",
    )(x, picks)


def inverse_factor(square, out):
    size = square.shape[0]
    groups = size // 8
    left = [square[8 * g:8 * g + 8, :] for g in range(groups)]
    lane = lax.broadcasted_iota(jnp.int32, (8, size), 1)
    row = lax.broadcasted_iota(jnp.int32, (8, size), 0)
    right = [(lane == row + 8 * g).astype(jnp.float32) for g in range(groups)]
    for g in range(groups):
        line, unit = left[g], right[g]
        spread = [
            jnp.broadcast_to(line[:, 8 * g + c:8 * g + c + 1], (8, size)) for c in range(8)
        ]
        scale = jnp.zeros((8, size), jnp.float32)
        for s in range(8):
            invert = 1.0 / spread[s][s:s + 1, :]
            scale = jnp.where(row == s, invert, scale)
            if s == 7:
                break
            factor = jnp.where(row > s, spread[s] * invert, 0.0)
            for c in range(s + 1, 8):
                spread[c] = spread[c] - factor * spread[c][s:s + 1, :]
            line = line - factor * line[s:s + 1, :]
            unit = unit - factor * unit[s:s + 1, :]
        out[8 * g:8 * g + 8, :] = unit * jnp.sqrt(scale)
        if g + 1 < groups:
            tail = dot(line, jnp.concatenate([line * scale, unit * scale], axis=1), ((0,), (0,)))
            for b in range(g + 1, groups):
                left[b] = left[b] - tail[8 * b:8 * b + 8, :size]
                right[b] = right[b] - tail[8 * b:8 * b + 8, size:]


def finish_kernel(scale, total_ref, panel_ref, x_ref, res_ref, basis_ref, inv1, inv2, inv, weights):
    @pl.when(pl.program_id(0) == 0)
    def _():
        n = LANES
        inverse_factor(total_ref[0:n, :], inv1)
        first = inv1[...]
        low = dot(total_ref[n:2 * n, :], first, ((1,), (1,)))
        rest = total_ref[4 * n:5 * n, :] - dot(low, low, ((1,), (1,)))
        inverse_factor(rest, inv2)
        second = inv2[...]
        inv[0:n, 0:n] = first
        inv[0:n, n:2 * n] = jnp.zeros((n, n), jnp.float32)
        inv[n:2 * n, 0:n] = -dot(second, dot(low, first))
        inv[n:2 * n, n:2 * n] = second
        weights[...] = dot(inv[...], total_ref[2 * n:4 * n, :])

    fresh = dot(panel_ref[...], inv[...], ((1,), (1,)))
    basis_ref[...] = fresh * scale
    res_ref[...] = x_ref[...] - dot(fresh, weights[...])


def finish(total, panel, x, scale, tile):
    rows, wide = panel.shape
    return pl.pallas_call(
        functools.partial(finish_kernel, scale),
        grid=(rows // tile,),
        out_shape=(
            jax.ShapeDtypeStruct(x.shape, jnp.float32),
            jax.ShapeDtypeStruct(panel.shape, jnp.float32),
        ),
        in_specs=[
            pl.BlockSpec(total.shape, lambda i: (0, 0)),
            pl.BlockSpec((tile, wide), lambda i: (i, 0)),
            pl.BlockSpec((tile, x.shape[1]), lambda i: (i, 0)),
        ],
        out_specs=[
            pl.BlockSpec((tile, x.shape[1]), lambda i: (i, 0)),
            pl.BlockSpec((tile, wide), lambda i: (i, 0)),
        ],
        scratch_shapes=[
            pltpu.VMEM((LANES, LANES), jnp.float32),
            pltpu.VMEM((LANES, LANES), jnp.float32),
            pltpu.VMEM((2 * LANES, 2 * LANES), jnp.float32),
            pltpu.VMEM((2 * LANES, LANES), jnp.float32),
        ],
        compiler_params=pltpu.CompilerParams(vmem_limit_bytes=24 * 2 ** 20),
        name="finish_basis",
    )(total, panel, x)


def solution(mesh):
    spaces, snaps = mesh.shape["space"], mesh.shape["snap"]

    def on_device(x, picks):
        rows = x.shape[0]
        panel, total = gather(x, picks.reshape(1, -1), spaces, snaps, 64)
        return finish(total, panel, x, math.sqrt(rows * spaces), 512)

    return jax.shard_map(
        on_device,
        mesh=mesh,
        in_specs=(P("space", "snap"), P()),
        out_specs=(P("space", "snap"), P("space", None)),
        check_vma=False,
    )
```

```python
import functools
import math

import jax
import jax.numpy as jnp
from jax import lax
from jax.experimental import pallas as pl
from jax.experimental.pallas import tpu as pltpu
from jax.sharding import PartitionSpec as P

MESH = pl.DeviceIdType.MESH
HIGHEST = lax.Precision.HIGHEST
LANES = 128


def dot(left, right, contract=((1,), (0,))):
    return lax.dot_general(
        left, right, (contract, ((), ())), precision=HIGHEST, preferred_element_type=jnp.float32
    )


def gather_kernel(
    spaces, snaps, chunk, block,
    x_ref, picks_ref, panel_ref, total_ref,
    own, acc, gram, parts,
    send_sem, recv_sem, gs_sem, gr_sem, bs_sem, br_sem,
):
    me = lax.axis_index("space")
    z = lax.axis_index("snap")
    rows = x_ref.shape[0]
    count = rows // chunk
    cols = x_ref.shape[1]
    column = lax.broadcasted_iota(jnp.int32, (cols, picks_ref.shape[1]), 0) + z * cols
    chosen = (column == picks_ref[...]).astype(jnp.float32)
    early = z // (snaps // 2)
    late = 1 - early

    barrier = pltpu.get_barrier_semaphore()
    for k in range(1, spaces):
        pl.semaphore_signal(
            barrier, inc=1, device_id={"space": lax.rem(me + k, spaces)}, device_id_type=MESH
        )
    for k in range(1, snaps):
        pl.semaphore_signal(
            barrier, inc=1, device_id={"snap": lax.rem(z + k, snaps)}, device_id_type=MESH
        )
    pl.semaphore_wait(barrier, spaces + snaps - 2)

    def span(c):
        return pl.ds(pl.multiple_of(c * chunk, chunk), chunk)

    def place(d):
        return z + d * (snaps - 1 - 2 * z)

    def hop(d, c):
        return pltpu.make_async_remote_copy(
            src_ref=acc.at[d, span(c)],
            dst_ref=acc.at[d, span(c)],
            send_sem=send_sem.at[d, c],
            recv_sem=recv_sem.at[d, c],
            device_id={"snap": lax.rem(z + 1 - 2 * d + snaps, snaps)},
            device_id_type=MESH,
        )

    @pl.when(place(early) == 0)
    def _():
        def prepare(c, carry):
            mine = dot(x_ref[span(c), :], chosen)
            acc[early, span(c), :] = mine
            hop(early, c).start()
            return carry

        lax.fori_loop(0, count, prepare, 0)

    gram[...] = jnp.zeros_like(gram)

    def relay(c):
        @pl.when(place(early) > 0)
        def _():
            mine = dot(x_ref[span(c), :], chosen)
            own[span(c), :] = mine
            hop(early, c).wait_recv()
            acc[early, span(c), :] = acc[early, span(c), :] + mine
            hop(early, c).start()

    def join(c):
        hop(late, c).wait_recv()
        came = acc[late, span(c), :]
        panel_ref[span(c), :] = came + acc[early, span(c), :]

        @pl.when(place(late) < snaps - 1)
        def _():
            acc[late, span(c), :] = came + own[span(c), :]
            hop(late, c).start()

    def square(pair):
        where = pl.ds(pl.multiple_of(pair * 2 * chunk, 2 * chunk), 2 * chunk)
        panel = panel_ref[where, :]
        half = panel.shape[1] // 2
        first, second = panel[:, :half], panel[:, half:]
        wide = jnp.concatenate([first, x_ref[where, :]], axis=1)
        both = dot(panel, wide, ((0,), (0,)))
        gram[0:2 * half, :] += both[:, :half]
        gram[2 * half:4 * half, :] += both[:, half:]
        gram[4 * half:5 * half, :] += dot(second, second, ((0,), (0,)))

    for c in range(4):
        relay(c)
    join(0)

    def step(t, carry):
        relay(2 * t)
        join(2 * t - 3)
        square(t - 2)
        relay(2 * t + 1)
        join(2 * t - 2)
        return carry

    lax.fori_loop(2, count // 2, step, 0)
    join(count - 3)
    square(count // 2 - 2)
    join(count - 2)
    join(count - 1)
    square(count // 2 - 1)

    def owned(k):
        return pl.ds(pl.multiple_of(k * block, block), block)

    def scatter(k):
        peer = lax.rem(me + k, spaces)
        return pltpu.make_async_remote_copy(
            src_ref=gram.at[owned(peer)],
            dst_ref=parts.at[k],
            send_sem=gs_sem.at[k],
            recv_sem=gr_sem.at[k],
            device_id={"space": peer},
            device_id_type=MESH,
        )

    def spread(k):
        return pltpu.make_async_remote_copy(
            src_ref=total_ref.at[owned(me)],
            dst_ref=total_ref.at[owned(me)],
            send_sem=bs_sem.at[k],
            recv_sem=br_sem.at[k],
            device_id={"space": lax.rem(me + k, spaces)},
            device_id_type=MESH,
        )

    for k in range(1, spaces):
        scatter(k).start()
    mine = gram[owned(me), :]
    for k in range(1, spaces):
        scatter(k).wait_recv()
        mine = mine + parts[k]
    total_ref[owned(me), :] = mine
    for k in range(1, spaces):
        spread(k).start()
    for k in range(1, spaces):
        source = lax.rem(me - k + spaces, spaces)
        pltpu.make_async_remote_copy(
            src_ref=total_ref.at[owned(me)],
            dst_ref=total_ref.at[owned(source)],
            send_sem=bs_sem.at[k],
            recv_sem=br_sem.at[k],
            device_id={"space": lax.rem(me + k, spaces)},
            device_id_type=MESH,
        ).wait_recv()
    for k in range(1, spaces):
        scatter(k).wait_send()
        spread(k).wait_send()

    def drain(c, carry):
        hop(early, c).wait_send()

        @pl.when(place(late) < snaps - 1)
        def _():
            hop(late, c).wait_send()

        return carry

    lax.fori_loop(0, count, drain, 0)


def gather(x, picks, spaces, snaps, chunk):
    rows, wide = x.shape[0], picks.shape[1]
    count = rows // chunk
    height = 5 * wide // 2
    block = -(-height // (8 * spaces)) * 8
    return pl.pallas_call(
        functools.partial(gather_kernel, spaces, snaps, chunk, block),
        out_shape=(
            jax.ShapeDtypeStruct((rows, wide), jnp.float32),
            jax.ShapeDtypeStruct((spaces * block, LANES), jnp.float32),
        ),
        in_specs=[pl.BlockSpec(memory_space=pltpu.VMEM)] * 2,
        out_specs=[pl.BlockSpec(memory_space=pltpu.VMEM)] * 2,
        scratch_shapes=[
            pltpu.VMEM((rows, wide), jnp.float32),
            pltpu.VMEM((2, rows, wide), jnp.float32),
            pltpu.VMEM((spaces * block, LANES), jnp.float32),
            pltpu.VMEM((spaces, block, LANES), jnp.float32),
            pltpu.SemaphoreType.DMA((2, count)),
            pltpu.SemaphoreType.DMA((2, count)),
            pltpu.SemaphoreType.DMA((spaces,)),
            pltpu.SemaphoreType.DMA((spaces,)),
            pltpu.SemaphoreType.DMA((spaces,)),
            pltpu.SemaphoreType.DMA((spaces,)),
        ],
        compiler_params=pltpu.CompilerParams(
            collective_id=0, has_side_effects=True, vmem_limit_bytes=40 * 2 ** 20
        ),
        name="gather_panel",
    )(x, picks)


def inverse_factor(square, out):
    size = square.shape[0]
    groups = size // 8
    left = [square[8 * g:8 * g + 8, :] for g in range(groups)]
    lane = lax.broadcasted_iota(jnp.int32, (8, size), 1)
    row = lax.broadcasted_iota(jnp.int32, (8, size), 0)
    right = [(lane == row + 8 * g).astype(jnp.float32) for g in range(groups)]
    for g in range(groups):
        line, unit = left[g], right[g]
        spread = [
            jnp.broadcast_to(line[:, 8 * g + c:8 * g + c + 1], (8, size)) for c in range(8)
        ]
        scale = jnp.zeros((8, size), jnp.float32)
        for s in range(8):
            invert = 1.0 / spread[s][s:s + 1, :]
            scale = jnp.where(row == s, invert, scale)
            if s == 7:
                break
            factor = jnp.where(row > s, spread[s] * invert, 0.0)
            for c in range(s + 1, 8):
                spread[c] = spread[c] - factor * spread[c][s:s + 1, :]
            line = line - factor * line[s:s + 1, :]
            unit = unit - factor * unit[s:s + 1, :]
        out[8 * g:8 * g + 8, :] = unit * jnp.sqrt(scale)
        if g + 1 < groups:
            tail = dot(line, jnp.concatenate([line * scale, unit * scale], axis=1), ((0,), (0,)))
            for b in range(g + 1, groups):
                left[b] = left[b] - tail[8 * b:8 * b + 8, :size]
                right[b] = right[b] - tail[8 * b:8 * b + 8, size:]


def split(value):
    high = value.astype(jnp.bfloat16)
    return high, (value - high.astype(jnp.float32)).astype(jnp.bfloat16)


def dot3(left, high, low):
    def part(a, b):
        return jnp.dot(a, b, preferred_element_type=jnp.float32)

    top, rest = split(left)
    return part(top, high) + (part(top, low) + part(rest, high))


def finish_kernel(
    scale, total_ref, panel_ref, x_ref, res_ref, basis_ref,
    inv1, inv2, inv, inv_high, inv_low, w_high, w_low,
):
    @pl.when(pl.program_id(0) == 0)
    def _():
        n = LANES
        inverse_factor(total_ref[0:n, :], inv1)
        first = inv1[...]
        low = dot(total_ref[n:2 * n, :], first, ((1,), (1,)))
        rest = total_ref[4 * n:5 * n, :] - dot(low, low, ((1,), (1,)))
        inverse_factor(rest, inv2)
        second = inv2[...]
        inv[0:n, 0:n] = first
        inv[0:n, n:2 * n] = jnp.zeros((n, n), jnp.float32)
        inv[n:2 * n, 0:n] = -dot(second, dot(low, first))
        inv[n:2 * n, n:2 * n] = second
        w_high[...], w_low[...] = split(dot(inv[...], total_ref[2 * n:4 * n, :]))
        inv_high[...], inv_low[...] = split(inv[...].T)

    fresh = dot3(panel_ref[...], inv_high[...], inv_low[...])
    basis_ref[...] = fresh * scale
    res_ref[...] = x_ref[...] - dot3(fresh, w_high[...], w_low[...])


def finish(total, panel, x, scale, tile):
    rows, wide = panel.shape
    return pl.pallas_call(
        functools.partial(finish_kernel, scale),
        grid=(rows // tile,),
        out_shape=(
            jax.ShapeDtypeStruct(x.shape, jnp.float32),
            jax.ShapeDtypeStruct(panel.shape, jnp.float32),
        ),
        in_specs=[
            pl.BlockSpec(total.shape, lambda i: (0, 0)),
            pl.BlockSpec((tile, wide), lambda i: (i, 0)),
            pl.BlockSpec((tile, x.shape[1]), lambda i: (i, 0)),
        ],
        out_specs=[
            pl.BlockSpec((tile, x.shape[1]), lambda i: (i, 0)),
            pl.BlockSpec((tile, wide), lambda i: (i, 0)),
        ],
        scratch_shapes=[
            pltpu.VMEM((LANES, LANES), jnp.float32),
            pltpu.VMEM((LANES, LANES), jnp.float32),
            pltpu.VMEM((2 * LANES, 2 * LANES), jnp.float32),
            pltpu.VMEM((2 * LANES, 2 * LANES), jnp.bfloat16),
            pltpu.VMEM((2 * LANES, 2 * LANES), jnp.bfloat16),
            pltpu.VMEM((2 * LANES, LANES), jnp.bfloat16),
            pltpu.VMEM((2 * LANES, LANES), jnp.bfloat16),
        ],
        compiler_params=pltpu.CompilerParams(vmem_limit_bytes=24 * 2 ** 20),
        name="finish_basis",
    )(total, panel, x)


def solution(mesh):
    spaces, snaps = mesh.shape["space"], mesh.shape["snap"]

    def on_device(x, picks):
        rows = x.shape[0]
        panel, total = gather(x, picks.reshape(1, -1), spaces, snaps, 64)
        return finish(total, panel, x, math.sqrt(rows * spaces), 512)

    return jax.shard_map(
        on_device,
        mesh=mesh,
        in_specs=(P("space", "snap"), P()),
        out_specs=(P("space", "snap"), P("space", None)),
        check_vma=False,
    )
```

```python
import functools
import math

import jax
import jax.numpy as jnp
from jax import lax
from jax.experimental import pallas as pl
from jax.experimental.pallas import tpu as pltpu
from jax.sharding import PartitionSpec as P

MESH = pl.DeviceIdType.MESH
HIGHEST = lax.Precision.HIGHEST
LANES = 128


def dot(left, right, contract=((1,), (0,))):
    return lax.dot_general(
        left, right, (contract, ((), ())), precision=HIGHEST, preferred_element_type=jnp.float32
    )


def gather_kernel(
    spaces, snaps, chunk, block,
    x_ref, picks_ref, panel_ref, total_ref,
    own, acc, gram, parts,
    send_sem, recv_sem, gs_sem, gr_sem, bs_sem, br_sem,
):
    me = lax.axis_index("space")
    z = lax.axis_index("snap")
    rows = x_ref.shape[0]
    count = rows // chunk
    cols = x_ref.shape[1]
    column = lax.broadcasted_iota(jnp.int32, (cols, picks_ref.shape[1]), 0) + z * cols
    chosen = (column == picks_ref[...]).astype(jnp.float32)
    early = z // (snaps // 2)
    late = 1 - early

    barrier = pltpu.get_barrier_semaphore()
    for k in range(1, spaces):
        pl.semaphore_signal(
            barrier, inc=1, device_id={"space": lax.rem(me + k, spaces)}, device_id_type=MESH
        )
    for k in range(1, snaps):
        pl.semaphore_signal(
            barrier, inc=1, device_id={"snap": lax.rem(z + k, snaps)}, device_id_type=MESH
        )
    pl.semaphore_wait(barrier, spaces + snaps - 2)

    def span(c):
        return pl.ds(pl.multiple_of(c * chunk, chunk), chunk)

    def place(d):
        return z + d * (snaps - 1 - 2 * z)

    def hop(d, c):
        return pltpu.make_async_remote_copy(
            src_ref=acc.at[d, span(c)],
            dst_ref=acc.at[d, span(c)],
            send_sem=send_sem.at[d, c],
            recv_sem=recv_sem.at[d, c],
            device_id={"snap": lax.rem(z + 1 - 2 * d + snaps, snaps)},
            device_id_type=MESH,
        )

    @pl.when(place(early) == 0)
    def _():
        def prepare(c, carry):
            mine = dot(x_ref[span(c), :], chosen)
            acc[early, span(c), :] = mine
            hop(early, c).start()
            return carry

        lax.fori_loop(0, count, prepare, 0)

    gram[...] = jnp.zeros_like(gram)

    def relay(c):
        @pl.when(place(early) > 0)
        def _():
            mine = dot(x_ref[span(c), :], chosen)
            own[span(c), :] = mine
            hop(early, c).wait_recv()
            acc[early, span(c), :] = acc[early, span(c), :] + mine
            hop(early, c).start()

    def join(c):
        hop(late, c).wait_recv()
        came = acc[late, span(c), :]
        panel_ref[span(c), :] = came + acc[early, span(c), :]

        @pl.when(place(late) < snaps - 1)
        def _():
            acc[late, span(c), :] = came + own[span(c), :]
            hop(late, c).start()

    def square(pair):
        where = pl.ds(pl.multiple_of(pair * 2 * chunk, 2 * chunk), 2 * chunk)
        panel = panel_ref[where, :]
        half = panel.shape[1] // 2
        first, second = panel[:, :half], panel[:, half:]
        wide = jnp.concatenate([first, x_ref[where, :]], axis=1)
        both = dot(panel, wide, ((0,), (0,)))
        gram[0:2 * half, :] += both[:, :half]
        gram[2 * half:4 * half, :] += both[:, half:]
        gram[4 * half:5 * half, :] += dot(second, second, ((0,), (0,)))

    for c in range(4):
        relay(c)
    join(0)

    def step(t, carry):
        relay(2 * t)
        join(2 * t - 3)
        square(t - 2)
        relay(2 * t + 1)
        join(2 * t - 2)
        return carry

    lax.fori_loop(2, count // 2, step, 0)
    join(count - 3)
    square(count // 2 - 2)
    join(count - 2)
    join(count - 1)
    square(count // 2 - 1)

    def owned(k):
        return pl.ds(pl.multiple_of(k * block, block), block)

    def scatter(k):
        peer = lax.rem(me + k, spaces)
        return pltpu.make_async_remote_copy(
            src_ref=gram.at[owned(peer)],
            dst_ref=parts.at[k],
            send_sem=gs_sem.at[k],
            recv_sem=gr_sem.at[k],
            device_id={"space": peer},
            device_id_type=MESH,
        )

    def spread(k):
        return pltpu.make_async_remote_copy(
            src_ref=total_ref.at[owned(me)],
            dst_ref=total_ref.at[owned(me)],
            send_sem=bs_sem.at[k],
            recv_sem=br_sem.at[k],
            device_id={"space": lax.rem(me + k, spaces)},
            device_id_type=MESH,
        )

    for k in range(1, spaces):
        scatter(k).start()
    mine = gram[owned(me), :]
    for k in range(1, spaces):
        scatter(k).wait_recv()
        mine = mine + parts[k]
    total_ref[owned(me), :] = mine
    for k in range(1, spaces):
        spread(k).start()
    for k in range(1, spaces):
        source = lax.rem(me - k + spaces, spaces)
        pltpu.make_async_remote_copy(
            src_ref=total_ref.at[owned(me)],
            dst_ref=total_ref.at[owned(source)],
            send_sem=bs_sem.at[k],
            recv_sem=br_sem.at[k],
            device_id={"space": lax.rem(me + k, spaces)},
            device_id_type=MESH,
        ).wait_recv()
    for k in range(1, spaces):
        scatter(k).wait_send()
        spread(k).wait_send()

    def drain(c, carry):
        hop(early, c).wait_send()

        @pl.when(place(late) < snaps - 1)
        def _():
            hop(late, c).wait_send()

        return carry

    lax.fori_loop(0, count, drain, 0)


def gather(x, picks, spaces, snaps, chunk):
    rows, wide = x.shape[0], picks.shape[1]
    count = rows // chunk
    height = 5 * wide // 2
    block = -(-height // (8 * spaces)) * 8
    return pl.pallas_call(
        functools.partial(gather_kernel, spaces, snaps, chunk, block),
        out_shape=(
            jax.ShapeDtypeStruct((rows, wide), jnp.float32),
            jax.ShapeDtypeStruct((spaces * block, LANES), jnp.float32),
        ),
        in_specs=[pl.BlockSpec(memory_space=pltpu.VMEM)] * 2,
        out_specs=[pl.BlockSpec(memory_space=pltpu.VMEM)] * 2,
        scratch_shapes=[
            pltpu.VMEM((rows, wide), jnp.float32),
            pltpu.VMEM((2, rows, wide), jnp.float32),
            pltpu.VMEM((spaces * block, LANES), jnp.float32),
            pltpu.VMEM((spaces, block, LANES), jnp.float32),
            pltpu.SemaphoreType.DMA((2, count)),
            pltpu.SemaphoreType.DMA((2, count)),
            pltpu.SemaphoreType.DMA((spaces,)),
            pltpu.SemaphoreType.DMA((spaces,)),
            pltpu.SemaphoreType.DMA((spaces,)),
            pltpu.SemaphoreType.DMA((spaces,)),
        ],
        compiler_params=pltpu.CompilerParams(
            collective_id=0, has_side_effects=True, vmem_limit_bytes=40 * 2 ** 20
        ),
        name="gather_panel",
    )(x, picks)


def inverse_factor(square, out):
    size = square.shape[0]
    groups = size // 8
    left = [square[8 * g:8 * g + 8, :] for g in range(groups)]
    lane = lax.broadcasted_iota(jnp.int32, (8, size), 1)
    row = lax.broadcasted_iota(jnp.int32, (8, size), 0)
    right = [(lane == row + 8 * g).astype(jnp.float32) for g in range(groups)]
    for g in range(groups):
        line, unit = left[g], right[g]
        spread = [
            jnp.broadcast_to(line[:, 8 * g + c:8 * g + c + 1], (8, size)) for c in range(8)
        ]
        scale = jnp.zeros((8, size), jnp.float32)
        for s in range(8):
            invert = 1.0 / spread[s][s:s + 1, :]
            scale = jnp.where(row == s, invert, scale)
            if s == 7:
                break
            factor = jnp.where(row > s, spread[s] * invert, 0.0)
            for c in range(s + 1, 8):
                spread[c] = spread[c] - factor * spread[c][s:s + 1, :]
            line = line - factor * line[s:s + 1, :]
            unit = unit - factor * unit[s:s + 1, :]
        out[8 * g:8 * g + 8, :] = unit * jnp.sqrt(scale)
        if g + 1 < groups:
            tail = dot(line, jnp.concatenate([line * scale, unit * scale], axis=1), ((0,), (0,)))
            for b in range(g + 1, groups):
                left[b] = left[b] - tail[8 * b:8 * b + 8, :size]
                right[b] = right[b] - tail[8 * b:8 * b + 8, size:]


def split(value):
    high = value.astype(jnp.bfloat16)
    return high, (value - high.astype(jnp.float32)).astype(jnp.bfloat16)


def dot3(left, high, low):
    def part(a, b):
        return jnp.dot(a, b, preferred_element_type=jnp.float32)

    top, rest = split(left)
    return part(top, high) + (part(top, low) + part(rest, high))


def finish_kernel(
    scale, total_ref, panel_ref, x_ref, res_ref, basis_ref,
    inv1, inv2, inv, high, low_part,
):
    @pl.when(pl.program_id(0) == 0)
    def _():
        n = LANES
        inverse_factor(total_ref[0:n, :], inv1)
        first = inv1[...]
        low = dot(total_ref[n:2 * n, :], first, ((1,), (1,)))
        rest = total_ref[4 * n:5 * n, :] - dot(low, low, ((1,), (1,)))
        inverse_factor(rest, inv2)
        second = inv2[...]
        inv[0:n, 0:n] = first
        inv[0:n, n:2 * n] = jnp.zeros((n, n), jnp.float32)
        inv[n:2 * n, 0:n] = -dot(second, dot(low, first))
        inv[n:2 * n, n:2 * n] = second
        turned = inv[...].T
        weights = dot(inv[...], total_ref[2 * n:4 * n, :])
        high[...], low_part[...] = split(jnp.concatenate([turned, dot(turned, weights)], axis=1))

    both = dot3(panel_ref[...], high[...], low_part[...])
    fresh = both[:, :2 * LANES]
    basis_ref[...] = fresh * scale
    res_ref[...] = x_ref[...] - both[:, 2 * LANES:]


def finish(total, panel, x, scale, tile):
    rows, wide = panel.shape
    return pl.pallas_call(
        functools.partial(finish_kernel, scale),
        grid=(rows // tile,),
        out_shape=(
            jax.ShapeDtypeStruct(x.shape, jnp.float32),
            jax.ShapeDtypeStruct(panel.shape, jnp.float32),
        ),
        in_specs=[
            pl.BlockSpec(total.shape, lambda i: (0, 0)),
            pl.BlockSpec((tile, wide), lambda i: (i, 0)),
            pl.BlockSpec((tile, x.shape[1]), lambda i: (i, 0)),
        ],
        out_specs=[
            pl.BlockSpec((tile, x.shape[1]), lambda i: (i, 0)),
            pl.BlockSpec((tile, wide), lambda i: (i, 0)),
        ],
        scratch_shapes=[
            pltpu.VMEM((LANES, LANES), jnp.float32),
            pltpu.VMEM((LANES, LANES), jnp.float32),
            pltpu.VMEM((2 * LANES, 2 * LANES), jnp.float32),
            pltpu.VMEM((2 * LANES, 3 * LANES), jnp.bfloat16),
            pltpu.VMEM((2 * LANES, 3 * LANES), jnp.bfloat16),
        ],
        compiler_params=pltpu.CompilerParams(vmem_limit_bytes=24 * 2 ** 20),
        name="finish_basis",
    )(total, panel, x)


def solution(mesh):
    spaces, snaps = mesh.shape["space"], mesh.shape["snap"]

    def on_device(x, picks):
        rows = x.shape[0]
        panel, total = gather(x, picks.reshape(1, -1), spaces, snaps, 64)
        return finish(total, panel, x, math.sqrt(rows * spaces), 1024)

    return jax.shard_map(
        on_device,
        mesh=mesh,
        in_specs=(P("space", "snap"), P()),
        out_specs=(P("space", "snap"), P("space", None)),
        check_vma=False,
    )
```
